32 devices in a mesh: dp: 8 (over y, x, core), blk: 4 (over z).
Axes of the slice: x: 2, y: 2, z: 4, core: 2. Of those that a mesh axis runs over, the one named last changes fastest.
Arguments:
- hidden_in: bfloat16 [768, 1152], P(('dp', 'blk')), may hold values from -6 to 6
- gain_mlp: float32 [1152], replicated, may hold values from 0.1 to 1.9
- gain_final: float32 [1152], replicated, may hold values from 0.1 to 1.9
- w_in: bfloat16 [1152, 4304], P(None, 'blk'), may hold values from -0.1875 to 0.1875
- w_out: bfloat16 [4304, 1152], P('blk'), may hold values from -0.09375 to 0.09375
- image_embeds: bfloat16 [768, 1152], P(('dp', 'blk')), may hold values from -6 to 6
- pair_ids: int32 [768], P(('dp', 'blk')), may hold values from 0 to 95
- teacher_logits: bfloat16 [8, 96, 96], P('dp', None, 'blk'), may hold values from -12 to 12
Outputs:
- grad_hidden: float32 [768, 1152], P(('dp', 'blk'))
- grad_w_in: float32 [1152, 4304], P(None, 'blk')
- grad_w_out: float32 [4304, 1152], P('blk')
The draws below stay inside these ranges and needn't reach their ends.
All inputs are finite; a program needn't handle non-finite values.
Results may differ from the reference program's by a relative error of at most 0.0067.
Values may be sent and summed in bfloat16 or wider, within the bound.
A program may use at most 64 MiB of HBM per device.

```python
import jax
import jax.numpy as jnp
from jax import lax

D = 1152
FF = 4304
G = 96
B = 768
N_DP = 8


def with_ends(entries, own_key, low, high):
    longest = entries.shape.index(max(entries.shape))
    spots = []
    for shift in (0, 1):
        where = [jax.random.randint(jax.random.fold_in(own_key, axis), (), 0, length) for axis, length in enumerate(entries.shape)]
        where[longest] = (where[longest] + shift) % entries.shape[longest]
        spots.append(tuple(where))
    return entries.at[spots[0]].set(low).at[spots[1]].set(high)


def level_of(stream_key, shape, pieces, smallest, high):
    level, own = 1.0, jax.random.fold_in(stream_key, 6)
    for dim, parts in pieces:
        steps = jnp.exp(jax.random.uniform(jax.random.fold_in(own, dim), (parts,), jnp.float32, smallest / len(pieces), high / len(pieces)))
        level = level * jnp.repeat(steps, shape[dim] // parts).reshape([-1 if axis == dim else 1 for axis in range(len(shape))])
    return level


def bell_draw(rng, extent, width, reach, split=(), dtype=jnp.bfloat16):
    values = jax.random.normal(rng, extent, jnp.float32) * width
    if len(split) > 0:
        values = level_of(rng, extent, split, -0.22, 0.18) * values
    return jnp.clip(values, min=-reach, max=reach).astype(dtype)


def setup_inputs(seed: int = 0) -> dict:
    key_list = jax.random.split(jax.random.key(seed), 9)
    return {
        "hidden_in": bell_draw(key_list[0], (B, D), 1.0, 6.0, ((0, 32),)),
        "gain_mlp": jnp.clip(1.0 + 0.18 * jax.random.normal(key_list[1], (D,), jnp.float32), 0.1, 1.9),
        "gain_final": jnp.clip(1.0 + 0.18 * jax.random.normal(key_list[2], (D,), jnp.float32), 0.1, 1.9),
        "w_in": bell_draw(key_list[3], (D, FF), D ** -0.5, 0.1875, ((1, 4),)),
        "w_out": bell_draw(key_list[4], (FF, D), FF ** -0.5, 0.09375, ((0, 4),)),
        "image_embeds": bell_draw(key_list[5], (B, D), 1.0, 6.0, ((0, 32),)),
        "pair_ids": with_ends(jax.random.randint(key_list[6], (B,), 0, G), jax.random.fold_in(key_list[6], 1), 0, G - 1).astype(jnp.int32),
        "teacher_logits": bell_draw(key_list[7], (N_DP, G, G), 3.0, 12.0, ((0, 8), (2, 4))),
    }


epsilon = 1e-06
logit_scale = 10.0
logit_bias = -2.0
gelu_coeff = 0.7978845608028654

def layer_norm(values, gain_vec):
    row_mean = lax.optimization_barrier(jnp.mean(values, axis=-1, keepdims=True))
    centred = values - row_mean
    variance = lax.optimization_barrier(jnp.mean(centred * centred, axis=-1, keepdims=True))
    inverse = lax.rsqrt(variance + epsilon)
    normed = centred * inverse
    return (normed, inverse, normed * gain_vec)

def norm_backward(grad_normed, normed, inverse):
    mean_grad = lax.optimization_barrier(jnp.mean(grad_normed, axis=-1, keepdims=True))
    mean_cross = lax.optimization_barrier(jnp.mean(grad_normed * normed, axis=-1, keepdims=True))
    return inverse * (grad_normed - mean_grad - normed * mean_cross)

def gelu_both(pre_act):
    inner_arg = gelu_coeff * (pre_act + 0.044715 * pre_act * pre_act * pre_act)
    tangent = jnp.tanh(inner_arg)
    gelu_value = 0.5 * pre_act * (1.0 + tangent)
    gelu_slope = 0.5 * (1.0 + tangent) + 0.5 * pre_act * (1.0 - tangent * tangent) * gelu_coeff * (1.0 + 3.0 * 0.044715 * pre_act * pre_act)
    return (gelu_value, gelu_slope)

def reference(hidden_in, gain_mlp, gain_final, w_in, w_out, image_embeds, pair_ids, teacher_logits):
    hidden = hidden_in.astype(jnp.float32)
    normed_in, inverse_in, scaled_in = layer_norm(hidden, gain_mlp)
    mlp_input = scaled_in.astype(jnp.bfloat16)
    pre_act = jnp.dot(mlp_input, w_in, preferred_element_type=jnp.float32)
    gelu_value, gelu_slope = gelu_both(pre_act)
    activation = gelu_value.astype(jnp.bfloat16)
    residual = hidden + jnp.dot(activation, w_out, preferred_element_type=jnp.float32)
    normed_out, inverse_out, final_out = layer_norm(residual, gain_final)
    length = jnp.sqrt(lax.optimization_barrier(jnp.sum(final_out * final_out, axis=-1, keepdims=True)) + epsilon)
    unit_text = final_out / length
    text_embed = unit_text.astype(jnp.bfloat16)
    image_float = image_embeds.astype(jnp.float32)
    image_unit = (image_float * lax.rsqrt(lax.optimization_barrier(jnp.sum(image_float * image_float, axis=-1, keepdims=True)) + epsilon)).astype(jnp.bfloat16)
    text_groups = text_embed.astype(jnp.float32).reshape(N_DP, G, D)
    image_groups = image_unit.astype(jnp.float32).reshape(N_DP, G, D)
    group_pairs = pair_ids.reshape(N_DP, G)
    logits = jnp.einsum('gid,gjd->gij', image_groups, text_groups) * logit_scale + logit_bias
    same_pair = (group_pairs[:, :, None] == group_pairs[:, None, :]).astype(jnp.float32)
    target = 0.5 * same_pair + 0.5 * jax.nn.sigmoid(teacher_logits.astype(jnp.float32))
    pair_grad = (jax.nn.sigmoid(logits) - target).astype(jnp.bfloat16)
    text_grad = logit_scale * jnp.einsum('gij,gid->gjd', pair_grad.astype(jnp.float32), image_groups)
    text_grad = text_grad.reshape(B, D)
    radial = lax.optimization_barrier(jnp.sum(unit_text * text_grad, axis=-1, keepdims=True))
    grad_final = (text_grad - unit_text * radial) / length
    grad_residual = norm_backward(grad_final * gain_final, normed_out, inverse_out)
    residual_rows = grad_residual.astype(jnp.bfloat16)
    grad_activation = jnp.dot(residual_rows, w_out.T, preferred_element_type=jnp.float32)
    grad_pre = (grad_activation * gelu_slope).astype(jnp.bfloat16)
    grad_w_out = jnp.dot(activation.T, residual_rows, preferred_element_type=jnp.float32)
    grad_w_in = jnp.dot(mlp_input.T, grad_pre, preferred_element_type=jnp.float32)
    grad_input_norm = jnp.dot(grad_pre, w_in.T, preferred_element_type=jnp.float32)
    grad_hidden = grad_residual + norm_backward(grad_input_norm * gain_mlp, normed_in, inverse_in)
    return (grad_hidden, grad_w_in, grad_w_out)
```

```python
import functools

import jax
import jax.numpy as jnp
from jax import lax
from jax.experimental import pallas as pl
from jax.experimental.pallas import tpu as pltpu
from jax.sharding import PartitionSpec as P

epsilon = 1e-06
logit_scale = 10.0
logit_bias = -2.0
gelu_coeff = 0.7978845608028654


def from_behind(x, axis, by):
    length = lax.axis_size(axis)
    return lax.ppermute(x, axis, [(i, (i + by) % length) for i in range(length)])


def layer_norm(values, gain_vec):
    row_mean = jnp.mean(values, axis=-1, keepdims=True)
    centred = values - row_mean
    variance = jnp.mean(centred * centred, axis=-1, keepdims=True)
    inverse = lax.rsqrt(variance + epsilon)
    normed = centred * inverse
    return (normed, inverse, normed * gain_vec)


def norm_backward(grad_normed, normed, inverse):
    mean_grad = jnp.mean(grad_normed, axis=-1, keepdims=True)
    mean_cross = jnp.mean(grad_normed * normed, axis=-1, keepdims=True)
    return inverse * (grad_normed - mean_grad - normed * mean_cross)


def gelu_both(pre_act):
    inner_arg = gelu_coeff * (pre_act + 0.044715 * pre_act * pre_act * pre_act)
    tangent = jnp.tanh(inner_arg)
    gelu_value = 0.5 * pre_act * (1.0 + tangent)
    gelu_slope = 0.5 * (1.0 + tangent) + 0.5 * pre_act * (1.0 - tangent * tangent) * gelu_coeff * (
        1.0 + 3.0 * 0.044715 * pre_act * pre_act
    )
    return (gelu_value, gelu_slope)


def tile_grad(image_rows, image_ids, text_rows, text_ids, teacher_tile):
    logits = lax.dot_general(
        image_rows, text_rows, (((1,), (1,)), ((), ())), preferred_element_type=jnp.float32
    )
    logits = logits * logit_scale + logit_bias
    same_pair = (image_ids[:, None] == text_ids[None, :]).astype(jnp.float32)
    target = 0.5 * same_pair + 0.5 * jax.nn.sigmoid(teacher_tile.astype(jnp.float32))
    pair_grad = (jax.nn.sigmoid(logits) - target).astype(jnp.bfloat16)
    return lax.dot_general(
        pair_grad, image_rows, (((0,), (0,)), ((), ())), preferred_element_type=jnp.float32
    )


def per_device(
    hidden_in, gain_mlp, gain_final, w_in, w_out, image_embeds, pair_ids, teacher_logits
):
    row_count = hidden_in.shape[0]
    width = hidden_in.shape[1]
    blocks = lax.axis_size("blk")
    own_index = lax.axis_index("blk")
    hidden = hidden_in.astype(jnp.float32)
    normed_in, inverse_in, scaled_in = layer_norm(hidden, gain_mlp)
    mlp_input = scaled_in.astype(jnp.bfloat16)
    group_input = lax.all_gather(mlp_input, "blk", axis=0, tiled=True)
    pre_act = jnp.dot(group_input, w_in, preferred_element_type=jnp.float32)
    gelu_value, gelu_slope = gelu_both(pre_act)
    activation = gelu_value.astype(jnp.bfloat16)
    piece = activation
    residual = hidden + lax.psum_scatter(
        jnp.dot(piece, w_out, preferred_element_type=jnp.float32),
        "blk",
        scatter_dimension=0,
        tiled=True,
    )
    normed_out, inverse_out, final_out = layer_norm(residual, gain_final)
    length = jnp.sqrt(jnp.sum(final_out * final_out, axis=-1, keepdims=True) + epsilon)
    unit_text = final_out / length
    text_embed = unit_text.astype(jnp.bfloat16)
    image_float = image_embeds.astype(jnp.float32)
    image_unit = (
        image_float
        * lax.rsqrt(jnp.sum(image_float * image_float, axis=-1, keepdims=True) + epsilon)
    ).astype(jnp.bfloat16)
    group_ids = lax.all_gather(pair_ids, "blk", axis=0, tiled=True)
    teacher_cols = teacher_logits[0]
    empty_grads = jnp.zeros((row_count, width), jnp.float32)

    def rotate_once(turn_index, loop_state):
        image_rows, text_grads = loop_state
        source = (own_index - turn_index + blocks) % blocks
        image_ids = lax.dynamic_slice_in_dim(group_ids, source * row_count, row_count, 0)
        teacher_tile = lax.dynamic_slice_in_dim(teacher_cols, source * row_count, row_count, 0)
        text_grads = text_grads + tile_grad(
            image_rows, image_ids, text_embed, pair_ids, teacher_tile
        )
        image_rows = from_behind(image_rows, "blk", 1)
        return (image_rows, text_grads)

    loop_state = lax.fori_loop(0, blocks, rotate_once, (image_unit, empty_grads))
    text_grad = logit_scale * loop_state[1]
    radial = jnp.sum(unit_text * text_grad, axis=-1, keepdims=True)
    grad_final = (text_grad - unit_text * radial) / length
    grad_residual = norm_backward(grad_final * gain_final, normed_out, inverse_out)
    residual_rows = grad_residual.astype(jnp.bfloat16)
    group_grads = lax.all_gather(residual_rows, "blk", axis=0, tiled=True)
    grad_activation = lax.dot_general(
        group_grads, w_out, (((1,), (1,)), ((), ())), preferred_element_type=jnp.float32
    )
    grad_pre = (grad_activation * gelu_slope).astype(jnp.bfloat16)
    part_w_out = lax.dot_general(
        activation, group_grads, (((0,), (0,)), ((), ())), preferred_element_type=jnp.float32
    )
    part_w_in = lax.dot_general(
        group_input, grad_pre, (((0,), (0,)), ((), ())), preferred_element_type=jnp.float32
    )
    piece = grad_pre
    grad_input_norm = lax.psum_scatter(
        lax.dot_general(piece, w_in, (((1,), (1,)), ((), ())), preferred_element_type=jnp.float32),
        "blk",
        scatter_dimension=0,
        tiled=True,
    )
    grad_w_in, grad_w_out = lax.psum((part_w_in, part_w_out), "dp")
    grad_hidden = grad_residual + norm_backward(grad_input_norm * gain_mlp, normed_in, inverse_in)
    return (grad_hidden, grad_w_in, grad_w_out)


def half_width(width):
    return -(-width // 256) * 128


def pack(rows):
    width = rows.shape[1]
    half = half_width(width)
    low, high = rows[-8:, :half], rows[-8:, half:]
    if width - half < half:
        high = jnp.concatenate([high, jnp.zeros((8, 2 * half - width), rows.dtype)], axis=1)
    side = jnp.concatenate([low, high], axis=0)
    if rows.shape[0] > 24:
        side = jnp.concatenate([side, jnp.zeros((rows.shape[0] - 24, half), rows.dtype)], axis=0)
    return jnp.concatenate([rows[:-8], side], axis=1).astype(jnp.bfloat16)


def unpack(slab, width):
    half = half_width(width)
    slab = slab.astype(jnp.float32)
    last = jnp.concatenate([slab[:8, width:], slab[8:16, width : 2 * width - half]], axis=1)
    return jnp.concatenate([slab[:, :width], last], axis=0)


def tiles_of(extent, size):
    return [(at, min(size, extent - at)) for at in range(0, extent, size)]


def group_kernel(
    blocks, chips,
    hidden_ref, gain_mlp_ref, gain_final_ref, w_in_hbm, w_out_hbm, image_ref, ids_ref, teacher_ref,
    grad_hidden_ref, all_x, all_a, all_r, all_p,
    w_in, w_out, slab_x, slab_i, slab_r, id_cols, out_1, in_1, out_2, in_2, partial,
    rows_f32, group_x, group_i, group_r, group_a, group_p, slope,
    load_sem, blk_send, blk_recv, chip_send, chip_recv, core_send, core_recv, own_sem,
):
    f32, bf16 = jnp.float32, jnp.bfloat16
    rows, width = hidden_ref.shape
    hidden_units = w_in.shape[1]
    dp, blk = lax.axis_index("dp"), lax.axis_index("blk")
    chip, core = dp // 2, dp % 2
    tile = 384

    loads = [
        pltpu.make_async_copy(w_in_hbm, w_in, load_sem.at[0]),
        pltpu.make_async_copy(w_out_hbm, w_out, load_sem.at[1]),
    ]
    for load in loads:
        load.start()

    def blk_peer(k):
        return lax.rem(blk + k, blocks)

    def chip_peer(k):
        return lax.rem(chip + k, chips) * 2 + core

    barrier = pltpu.get_barrier_semaphore()
    for k in range(1, blocks):
        pl.semaphore_signal(barrier, inc=1, device_id={"dp": dp, "blk": blk_peer(k)})
    for k in range(1, chips):
        pl.semaphore_signal(barrier, inc=1, device_id={"dp": chip_peer(k), "blk": blk})
    pl.semaphore_signal(barrier, inc=1, device_id={"dp": chip * 2 + 1 - core, "blk": blk})

    sends = []

    def blk_copy(phase, k, src, dst):
        return pltpu.make_async_remote_copy(
            src_ref=src, dst_ref=dst, send_sem=blk_send.at[phase, k - 1], recv_sem=blk_recv.at[phase, k - 1],
            device_id={"dp": dp, "blk": blk_peer(k)},
        )

    def share(phase, buffer):
        copies = [blk_copy(phase, k, buffer.at[blk], buffer.at[blk]) for k in range(1, blocks)]
        for copy in copies:
            copy.start()
        sends.extend(copies)
        return copies

    def arrived(copies):
        for copy in copies:
            copy.wait_recv()

    def spread(kind, source, landing):
        copies = []
        for k in range(1, chips):
            copies.append(pltpu.make_async_remote_copy(
                src_ref=source, dst_ref=landing.at[dp], send_sem=chip_send.at[kind, k - 1],
                recv_sem=chip_recv.at[kind, k - 1], device_id={"dp": chip_peer(k), "blk": blk},
            ))
        other = pltpu.make_async_remote_copy(
            src_ref=source, dst_ref=landing.at[dp], send_sem=core_send.at[kind, 0],
            recv_sem=core_recv.at[kind, 0], device_id={"dp": chip * 2 + 1 - core, "blk": blk},
        )
        own = pltpu.make_async_copy(source, landing.at[dp], own_sem.at[kind])
        for copy in copies + [other, own]:
            copy.start()
        sends.extend(copies + [other])
        return copies, [other], own

    def relay(kind, landing, state):
        copies, others, own = state
        for k in range(1, chips):
            copies[k - 1].wait_recv()
            place = landing.at[lax.rem(chip + chips - k, chips) * 2 + core]
            other = pltpu.make_async_remote_copy(
                src_ref=place, dst_ref=place, send_sem=core_send.at[kind, k],
                recv_sem=core_recv.at[kind, k], device_id={"dp": chip * 2 + 1 - core, "blk": blk},
            )
            other.start()
            others.append(other)
            sends.append(other)

    def finish(state):
        arrived(state[1])
        state[2].wait()

    def regroup(buffer, target):
        for j in range(blocks):
            rows_f32[j * rows : (j + 1) * rows, :] = unpack(buffer[j], width)
        for at, size in tiles_of(width, tile):
            target[:, at : at + size] = rows_f32[:, at : at + size].astype(bf16)

    def scatter(phase, out_buf, in_buf):
        for k in range(1, blocks):
            out_buf[k - 1] = pack(partial[pl.ds(pl.multiple_of(blk_peer(k) * rows, 8), rows), :])
        copies = [blk_copy(phase, k, out_buf.at[k - 1], in_buf.at[k - 1]) for k in range(1, blocks)]
        for copy in copies:
            copy.start()
        sends.extend(copies)
        return copies

    def collect(copies, in_buf):
        total = partial[pl.ds(pl.multiple_of(blk * rows, 8), rows), :]
        for k in range(1, blocks):
            copies[k - 1].wait_recv()
            total = total + unpack(in_buf[k - 1], width)
        return total

    hidden = hidden_ref[...].astype(f32)
    normed_in, inverse_in, scaled_in = layer_norm(hidden, gain_mlp_ref[...])
    slab_x[blk] = pack(scaled_in.astype(bf16).astype(f32))
    pl.semaphore_wait(barrier, blocks - 1 + chips - 1 + 1)
    came_x = share(0, slab_x)

    image = image_ref[...].astype(f32)
    image = image * lax.rsqrt(jnp.sum(image * image, axis=-1, keepdims=True) + epsilon)
    slab_i[blk] = pack(image.astype(bf16).astype(f32))
    square = (rows, rows)
    diagonal = lax.broadcasted_iota(jnp.int32, square, 0) == lax.broadcasted_iota(jnp.int32, square, 1)
    own_ids = ids_ref[...]
    column = jnp.sum(jnp.where(diagonal, own_ids, 0), axis=1, keepdims=True)
    id_cols[blk] = jnp.broadcast_to(column, id_cols.shape[1:])
    came_i = share(1, slab_i)
    came_ids = share(2, id_cols)

    arrived(came_x)
    regroup(slab_x, group_x)
    dp_x = spread(0, group_x, all_x)
    loads[0].wait()
    for at, size in tiles_of(hidden_units, tile):
        pre_act = jnp.dot(group_x[...], w_in[:, at : at + size], preferred_element_type=f32)
        value, steep = gelu_both(pre_act)
        group_a[:, at : at + size] = value.astype(bf16)
        slope[:, at : at + size] = steep
    dp_a = spread(1, group_a, all_a)
    loads[1].wait()
    for at, size in tiles_of(width, tile):
        partial[:, at : at + size] = jnp.dot(group_a[...], w_out[:, at : at + size], preferred_element_type=f32)
    sums_1 = scatter(3, out_1, in_1)

    arrived(came_i)
    arrived(came_ids)
    regroup(slab_i, group_i)
    eye = diagonal.astype(bf16)
    teacher = jax.nn.sigmoid(teacher_ref[0].astype(f32))
    image_ids = jnp.concatenate([id_cols[j][:, :1] for j in range(blocks)], axis=0)
    same_pair = (image_ids == own_ids).astype(f32)
    target = 0.5 * same_pair + 0.5 * teacher

    residual = hidden + collect(sums_1, in_1)
    normed_out, inverse_out, final_out = layer_norm(residual, gain_final_ref[...])
    length = jnp.sqrt(jnp.sum(final_out * final_out, axis=-1, keepdims=True) + epsilon)
    unit_text = final_out / length
    last_dims = (((1,), (1,)), ((), ()))
    logits = lax.dot_general(group_i[...], unit_text.astype(bf16), last_dims, preferred_element_type=f32)
    logits = logits * logit_scale + logit_bias
    pair_grad = (jax.nn.sigmoid(logits) - target).astype(bf16)
    turned = lax.dot_general(eye, pair_grad, last_dims, preferred_element_type=f32).astype(bf16)
    text_grad = logit_scale * jnp.dot(turned, group_i[...], preferred_element_type=f32)
    radial = jnp.sum(unit_text * text_grad, axis=-1, keepdims=True)
    grad_final = (text_grad - unit_text * radial) / length
    grad_residual = norm_backward(grad_final * gain_final_ref[...], normed_out, inverse_out)
    slab_r[blk] = pack(grad_residual.astype(bf16).astype(f32))
    came_r = share(4, slab_r)
    relay(0, all_x, dp_x)
    arrived(came_r)
    regroup(slab_r, group_r)
    dp_r = spread(2, group_r, all_r)
    for at, size in tiles_of(hidden_units, tile):
        grad_act = lax.dot_general(group_r[...], w_out[at : at + size, :], last_dims, preferred_element_type=f32)
        group_p[:, at : at + size] = (grad_act * slope[:, at : at + size]).astype(bf16)
    dp_p = spread(3, group_p, all_p)
    for at, size in tiles_of(width, tile):
        partial[:, at : at + size] = lax.dot_general(
            group_p[...], w_in[at : at + size, :], last_dims, preferred_element_type=f32
        )
    sums_2 = scatter(5, out_2, in_2)
    relay(1, all_a, dp_a)
    grad_norm = collect(sums_2, in_2)
    grad_hidden_ref[...] = grad_residual + norm_backward(grad_norm * gain_mlp_ref[...], normed_in, inverse_in)
    relay(2, all_r, dp_r)
    relay(3, all_p, dp_p)
    for state in (dp_x, dp_a, dp_r, dp_p):
        finish(state)
    for copy in sends:
        copy.wait_send()


def gathered_device(
    hidden_in, gain_mlp, gain_final, w_in, w_out, image_embeds, pair_ids, teacher_logits
):
    rows, width = hidden_in.shape
    units = w_in.shape[1]
    blocks, groups = lax.axis_size("blk"), lax.axis_size("dp")
    chips = groups // 2
    group = rows * blocks
    f32, bf16 = jnp.float32, jnp.bfloat16
    packed = (16 * (rows // 16), width + half_width(width))
    vmem, anywhere = pl.BlockSpec(memory_space=pltpu.VMEM), pl.BlockSpec(memory_space=pl.ANY)
    dma = pltpu.SemaphoreType.DMA
    grad_hidden, all_x, all_a, all_r, all_p = pl.pallas_call(
        functools.partial(group_kernel, blocks, chips),
        out_shape=(
            jax.ShapeDtypeStruct((rows, width), f32),
            jax.ShapeDtypeStruct((groups, group, width), bf16),
            jax.ShapeDtypeStruct((groups, group, units), bf16),
            jax.ShapeDtypeStruct((groups, group, width), bf16),
            jax.ShapeDtypeStruct((groups, group, units), bf16),
        ),
        in_specs=[vmem, vmem, vmem, anywhere, anywhere, vmem, vmem, vmem],
        out_specs=(vmem, anywhere, anywhere, anywhere, anywhere),
        scratch_shapes=[
            pltpu.VMEM(w_in.shape, bf16),
            pltpu.VMEM(w_out.shape, bf16),
            pltpu.VMEM((blocks,) + packed, bf16),
            pltpu.VMEM((blocks,) + packed, bf16),
            pltpu.VMEM((blocks,) + packed, bf16),
            pltpu.VMEM((blocks, rows, 128), jnp.int32),
            pltpu.VMEM((blocks - 1,) + packed, bf16),
            pltpu.VMEM((blocks - 1,) + packed, bf16),
            pltpu.VMEM((blocks - 1,) + packed, bf16),
            pltpu.VMEM((blocks - 1,) + packed, bf16),
            pltpu.VMEM((group, width), f32),
            pltpu.VMEM((group, width), f32),
            pltpu.VMEM((group, width), bf16),
            pltpu.VMEM((group, width), bf16),
            pltpu.VMEM((group, width), bf16),
            pltpu.VMEM((group, units), bf16),
            pltpu.VMEM((group, units), bf16),
            pltpu.VMEM((group, units), f32),
            dma((2,)),
            dma((6, blocks - 1)),
            dma((6, blocks - 1)),
            dma((4, chips - 1)),
            dma((4, chips - 1)),
            dma((4, chips)),
            dma((4, chips)),
            dma((4,)),
        ],
        compiler_params=pltpu.CompilerParams(
            collective_id=0, has_side_effects=True, vmem_limit_bytes=40 * 1024 * 1024
        ),
    )(
        hidden_in, gain_mlp[None, :], gain_final[None, :], w_in, w_out, image_embeds, pair_ids[None, :], teacher_logits
    )
    all_x, all_a, all_r, all_p = (v.reshape(groups * group, -1) for v in (all_x, all_a, all_r, all_p))
    over_rows = (((0,), (0,)), ((), ()))
    grad_w_out = lax.dot_general(all_a, all_r, over_rows, preferred_element_type=f32)
    grad_w_in = lax.dot_general(all_x, all_p, over_rows, preferred_element_type=f32)
    return grad_hidden, grad_w_in, grad_w_out


def choose(*args):
    rows, width = args[0].shape
    units = args[3].shape[1]
    groups, blocks = lax.axis_size("dp"), lax.axis_size("blk")
    gathered = groups * blocks * rows * (width + units) * 2 * 2
    summed = width * units * 2 * 4
    fits = groups % 2 == 0 and groups > 2 and blocks > 1 and rows % 16 == 8 and rows > 16 and width % 128 == 0
    if fits and gathered <= summed:
        return gathered_device(*args)
    return per_device(*args)


def solution(mesh):
    in_specs = (
        P(("dp", "blk"), None),
        P(),
        P(),
        P(None, "blk"),
        P("blk", None),
        P(("dp", "blk"), None),
        P(("dp", "blk")),
        P("dp", None, "blk"),
    )
    out_specs = (P(("dp", "blk"), None), P(None, "blk"), P("blk", None))
    return jax.shard_map(
        choose, mesh=mesh, in_specs=in_specs, out_specs=out_specs, check_vma=False
    )
```

```python
import functools

import jax
import jax.numpy as jnp
from jax import lax
from jax.experimental import pallas as pl
from jax.experimental.pallas import tpu as pltpu
from jax.sharding import PartitionSpec as P

epsilon = 1e-06
logit_scale = 10.0
logit_bias = -2.0
gelu_coeff = 0.7978845608028654


def from_behind(x, axis, by):
    length = lax.axis_size(axis)
    return lax.ppermute(x, axis, [(i, (i + by) % length) for i in range(length)])


def layer_norm(values, gain_vec):
    row_mean = jnp.mean(values, axis=-1, keepdims=True)
    centred = values - row_mean
    variance = jnp.mean(centred * centred, axis=-1, keepdims=True)
    inverse = lax.rsqrt(variance + epsilon)
    normed = centred * inverse
    return (normed, inverse, normed * gain_vec)


def norm_backward(grad_normed, normed, inverse):
    mean_grad = jnp.mean(grad_normed, axis=-1, keepdims=True)
    mean_cross = jnp.mean(grad_normed * normed, axis=-1, keepdims=True)
    return inverse * (grad_normed - mean_grad - normed * mean_cross)


def gelu_both(pre_act):
    inner_arg = gelu_coeff * (pre_act + 0.044715 * pre_act * pre_act * pre_act)
    tangent = jnp.tanh(inner_arg)
    gelu_value = 0.5 * pre_act * (1.0 + tangent)
    gelu_slope = 0.5 * (1.0 + tangent) + 0.5 * pre_act * (1.0 - tangent * tangent) * gelu_coeff * (
        1.0 + 3.0 * 0.044715 * pre_act * pre_act
    )
    return (gelu_value, gelu_slope)


def tile_grad(image_rows, image_ids, text_rows, text_ids, teacher_tile):
    logits = lax.dot_general(
        image_rows, text_rows, (((1,), (1,)), ((), ())), preferred_element_type=jnp.float32
    )
    logits = logits * logit_scale + logit_bias
    same_pair = (image_ids[:, None] == text_ids[None, :]).astype(jnp.float32)
    target = 0.5 * same_pair + 0.5 * jax.nn.sigmoid(teacher_tile.astype(jnp.float32))
    pair_grad = (jax.nn.sigmoid(logits) - target).astype(jnp.bfloat16)
    return lax.dot_general(
        pair_grad, image_rows, (((0,), (0,)), ((), ())), preferred_element_type=jnp.float32
    )


def per_device(
    hidden_in, gain_mlp, gain_final, w_in, w_out, image_embeds, pair_ids, teacher_logits
):
    row_count = hidden_in.shape[0]
    width = hidden_in.shape[1]
    blocks = lax.axis_size("blk")
    own_index = lax.axis_index("blk")
    hidden = hidden_in.astype(jnp.float32)
    normed_in, inverse_in, scaled_in = layer_norm(hidden, gain_mlp)
    mlp_input = scaled_in.astype(jnp.bfloat16)
    group_input = lax.all_gather(mlp_input, "blk", axis=0, tiled=True)
    pre_act = jnp.dot(group_input, w_in, preferred_element_type=jnp.float32)
    gelu_value, gelu_slope = gelu_both(pre_act)
    activation = gelu_value.astype(jnp.bfloat16)
    piece = activation
    residual = hidden + lax.psum_scatter(
        jnp.dot(piece, w_out, preferred_element_type=jnp.float32),
        "blk",
        scatter_dimension=0,
        tiled=True,
    )
    normed_out, inverse_out, final_out = layer_norm(residual, gain_final)
    length = jnp.sqrt(jnp.sum(final_out * final_out, axis=-1, keepdims=True) + epsilon)
    unit_text = final_out / length
    text_embed = unit_text.astype(jnp.bfloat16)
    image_float = image_embeds.astype(jnp.float32)
    image_unit = (
        image_float
        * lax.rsqrt(jnp.sum(image_float * image_float, axis=-1, keepdims=True) + epsilon)
    ).astype(jnp.bfloat16)
    group_ids = lax.all_gather(pair_ids, "blk", axis=0, tiled=True)
    teacher_cols = teacher_logits[0]
    empty_grads = jnp.zeros((row_count, width), jnp.float32)

    def rotate_once(turn_index, loop_state):
        image_rows, text_grads = loop_state
        source = (own_index - turn_index + blocks) % blocks
        image_ids = lax.dynamic_slice_in_dim(group_ids, source * row_count, row_count, 0)
        teacher_tile = lax.dynamic_slice_in_dim(teacher_cols, source * row_count, row_count, 0)
        text_grads = text_grads + tile_grad(
            image_rows, image_ids, text_embed, pair_ids, teacher_tile
        )
        image_rows = from_behind(image_rows, "blk", 1)
        return (image_rows, text_grads)

    loop_state = lax.fori_loop(0, blocks, rotate_once, (image_unit, empty_grads))
    text_grad = logit_scale * loop_state[1]
    radial = jnp.sum(unit_text * text_grad, axis=-1, keepdims=True)
    grad_final = (text_grad - unit_text * radial) / length
    grad_residual = norm_backward(grad_final * gain_final, normed_out, inverse_out)
    residual_rows = grad_residual.astype(jnp.bfloat16)
    group_grads = lax.all_gather(residual_rows, "blk", axis=0, tiled=True)
    grad_activation = lax.dot_general(
        group_grads, w_out, (((1,), (1,)), ((), ())), preferred_element_type=jnp.float32
    )
    grad_pre = (grad_activation * gelu_slope).astype(jnp.bfloat16)
    part_w_out = lax.dot_general(
        activation, group_grads, (((0,), (0,)), ((), ())), preferred_element_type=jnp.float32
    )
    part_w_in = lax.dot_general(
        group_input, grad_pre, (((0,), (0,)), ((), ())), preferred_element_type=jnp.float32
    )
    piece = grad_pre
    grad_input_norm = lax.psum_scatter(
        lax.dot_general(piece, w_in, (((1,), (1,)), ((), ())), preferred_element_type=jnp.float32),
        "blk",
        scatter_dimension=0,
        tiled=True,
    )
    grad_w_in, grad_w_out = lax.psum((part_w_in, part_w_out), "dp")
    grad_hidden = grad_residual + norm_backward(grad_input_norm * gain_mlp, normed_in, inverse_in)
    return (grad_hidden, grad_w_in, grad_w_out)


def half_width(width):
    return -(-width // 256) * 128


def pack(rows):
    width = rows.shape[1]
    half = half_width(width)
    low, high = rows[-8:, :half], rows[-8:, half:]
    if width - half < half:
        high = jnp.concatenate([high, jnp.zeros((8, 2 * half - width), rows.dtype)], axis=1)
    side = jnp.concatenate([low, high], axis=0)
    if rows.shape[0] > 24:
        side = jnp.concatenate([side, jnp.zeros((rows.shape[0] - 24, half), rows.dtype)], axis=0)
    return jnp.concatenate([rows[:-8], side], axis=1).astype(jnp.bfloat16)


def unpack(slab, width):
    half = half_width(width)
    slab = slab.astype(jnp.float32)
    last = jnp.concatenate([slab[:8, width:], slab[8:16, width : 2 * width - half]], axis=1)
    return jnp.concatenate([slab[:, :width], last], axis=0)


def tiles_of(extent, size):
    return [(at, min(size, extent - at)) for at in range(0, extent, size)]


def group_kernel(
    blocks, chips,
    hidden_ref, gain_mlp_ref, gain_final_ref, w_in_hbm, w_out_hbm, image_ref, ids_ref, teacher_ref,
    grad_hidden_ref, all_x, all_a, all_r, all_p,
    w_in, w_out, slab_x, slab_i, slab_r, id_rows, out_1, in_1, out_2, in_2, partial,
    rows_f32, group_x, group_i, group_r, group_a, group_p, slope,
    load_sem, blk_send, blk_recv, chip_send, chip_recv, core_send, core_recv, own_sem,
):
    f32, bf16 = jnp.float32, jnp.bfloat16
    rows, width = hidden_ref.shape
    hidden_units = w_in.shape[0]
    last_dims = (((1,), (1,)), ((), ()))
    dp, blk = lax.axis_index("dp"), lax.axis_index("blk")
    chip, core = dp // 2, dp % 2
    tile = 384

    loads = [
        pltpu.make_async_copy(w_in_hbm, w_in, load_sem.at[0]),
        pltpu.make_async_copy(w_out_hbm, w_out, load_sem.at[1]),
    ]
    for load in loads:
        load.start()

    def blk_peer(k):
        return lax.rem(blk + k, blocks)

    def chip_peer(k):
        return lax.rem(chip + k, chips) * 2 + core

    barrier = pltpu.get_barrier_semaphore()
    for k in range(1, blocks):
        pl.semaphore_signal(barrier, inc=1, device_id={"dp": dp, "blk": blk_peer(k)})
    for k in range(1, chips):
        pl.semaphore_signal(barrier, inc=1, device_id={"dp": chip_peer(k), "blk": blk})
    pl.semaphore_signal(barrier, inc=1, device_id={"dp": chip * 2 + 1 - core, "blk": blk})

    sends = []

    def blk_copy(phase, k, src, dst):
        return pltpu.make_async_remote_copy(
            src_ref=src, dst_ref=dst, send_sem=blk_send.at[phase, k - 1], recv_sem=blk_recv.at[phase, k - 1],
            device_id={"dp": dp, "blk": blk_peer(k)},
        )

    def share(phase, buffer):
        copies = [blk_copy(phase, k, buffer.at[blk], buffer.at[blk]) for k in range(1, blocks)]
        for copy in copies:
            copy.start()
        sends.extend(copies)
        return copies

    def arrived(copies):
        for copy in copies:
            copy.wait_recv()

    def spread(kind, source, landing):
        copies = []
        for k in range(1, chips):
            copies.append(pltpu.make_async_remote_copy(
                src_ref=source, dst_ref=landing.at[dp], send_sem=chip_send.at[kind, k - 1],
                recv_sem=chip_recv.at[kind, k - 1], device_id={"dp": chip_peer(k), "blk": blk},
            ))
        other = pltpu.make_async_remote_copy(
            src_ref=source, dst_ref=landing.at[dp], send_sem=core_send.at[kind, 0],
            recv_sem=core_recv.at[kind, 0], device_id={"dp": chip * 2 + 1 - core, "blk": blk},
        )
        own = pltpu.make_async_copy(source, landing.at[dp], own_sem.at[kind])
        for copy in copies + [other, own]:
            copy.start()
        sends.extend(copies + [other])
        return copies, [other], own

    def relay(kind, landing, state):
        copies, others, own = state
        for k in range(1, chips):
            copies[k - 1].wait_recv()
            place = landing.at[lax.rem(chip + chips - k, chips) * 2 + core]
            other = pltpu.make_async_remote_copy(
                src_ref=place, dst_ref=place, send_sem=core_send.at[kind, k],
                recv_sem=core_recv.at[kind, k], device_id={"dp": chip * 2 + 1 - core, "blk": blk},
            )
            other.start()
            others.append(other)
            sends.append(other)

    def finish(state):
        arrived(state[1])
        state[2].wait()

    def regroup(buffer, target):
        for j in range(blocks):
            rows_f32[j * rows : (j + 1) * rows, :] = unpack(buffer[j], width)
        for at, size in tiles_of(width, tile):
            target[:, at : at + size] = rows_f32[:, at : at + size].astype(bf16)

    def scatter(phase, out_buf, in_buf):
        for k in range(1, blocks):
            out_buf[k - 1] = pack(partial[pl.ds(pl.multiple_of(blk_peer(k) * rows, 8), rows), :])
        copies = [blk_copy(phase, k, out_buf.at[k - 1], in_buf.at[k - 1]) for k in range(1, blocks)]
        for copy in copies:
            copy.start()
        sends.extend(copies)
        return copies

    def collect(copies, in_buf):
        total = partial[pl.ds(pl.multiple_of(blk * rows, 8), rows), :]
        for k in range(1, blocks):
            copies[k - 1].wait_recv()
            total = total + unpack(in_buf[k - 1], width)
        return total

    hidden = hidden_ref[...].astype(f32)
    normed_in, inverse_in, scaled_in = layer_norm(hidden, gain_mlp_ref[...])
    slab_x[blk] = pack(scaled_in.astype(bf16).astype(f32))
    pl.semaphore_wait(barrier, blocks - 1 + chips - 1 + 1)
    came_x = share(0, slab_x)

    image = image_ref[...].astype(f32)
    image = image * lax.rsqrt(jnp.sum(image * image, axis=-1, keepdims=True) + epsilon)
    slab_i[blk] = pack(image.astype(bf16).astype(f32))
    square = (rows, rows)
    diagonal = lax.broadcasted_iota(jnp.int32, square, 0) == lax.broadcasted_iota(jnp.int32, square, 1)
    own_ids = ids_ref[...]
    column = jnp.sum(jnp.where(diagonal, own_ids, 0), axis=1, keepdims=True)
    id_rows[blk] = jnp.broadcast_to(jnp.concatenate([own_ids, jnp.zeros((1, 128 - rows), jnp.int32)], axis=1), id_rows.shape[1:])
    came_i = share(1, slab_i)
    came_ids = share(2, id_rows)

    arrived(came_x)
    regroup(slab_x, group_x)
    dp_x = spread(0, group_x, all_x)
    loads[0].wait()
    for at, size in tiles_of(hidden_units, tile):
        pre_act = lax.dot_general(
            group_x[...], w_in[at : at + size, :], last_dims, preferred_element_type=f32
        )
        value, steep = gelu_both(pre_act)
        group_a[:, at : at + size] = value.astype(bf16)
        slope[:, at : at + size] = steep
    dp_a = spread(1, group_a, all_a)
    loads[1].wait()
    for at, size in tiles_of(width, tile):
        partial[:, at : at + size] = jnp.dot(group_a[...], w_out[:, at : at + size], preferred_element_type=f32)
    sums_1 = scatter(3, out_1, in_1)

    arrived(came_i)
    arrived(came_ids)
    regroup(slab_i, group_i)
    teacher = jax.nn.sigmoid(teacher_ref[0].astype(f32))
    image_ids = jnp.concatenate([id_rows[j][:1, :rows] for j in range(blocks)], axis=1)
    same_pair = (image_ids == column).astype(f32)
    target = 0.5 * same_pair + 0.5 * teacher

    residual = hidden + collect(sums_1, in_1)
    normed_out, inverse_out, final_out = layer_norm(residual, gain_final_ref[...])
    length = jnp.sqrt(jnp.sum(final_out * final_out, axis=-1, keepdims=True) + epsilon)
    unit_text = final_out / length
    logits = lax.dot_general(unit_text.astype(bf16), group_i[...], last_dims, preferred_element_type=f32)
    logits = logits * logit_scale + logit_bias
    pair_grad = (jax.nn.sigmoid(logits) - target).astype(bf16)
    text_grad = logit_scale * jnp.dot(pair_grad, group_i[...], preferred_element_type=f32)
    radial = jnp.sum(unit_text * text_grad, axis=-1, keepdims=True)
    grad_final = (text_grad - unit_text * radial) / length
    grad_residual = norm_backward(grad_final * gain_final_ref[...], normed_out, inverse_out)
    slab_r[blk] = pack(grad_residual.astype(bf16).astype(f32))
    came_r = share(4, slab_r)
    relay(0, all_x, dp_x)
    arrived(came_r)
    regroup(slab_r, group_r)
    dp_r = spread(2, group_r, all_r)
    for at, size in tiles_of(hidden_units, tile):
        grad_act = lax.dot_general(group_r[...], w_out[at : at + size, :], last_dims, preferred_element_type=f32)
        group_p[:, at : at + size] = (grad_act * slope[:, at : at + size]).astype(bf16)
    dp_p = spread(3, group_p, all_p)
    for at, size in tiles_of(width, tile):
        partial[:, at : at + size] = jnp.dot(group_p[...], w_in[:, at : at + size], preferred_element_type=f32)
    sums_2 = scatter(5, out_2, in_2)
    relay(1, all_a, dp_a)
    grad_norm = collect(sums_2, in_2)
    grad_hidden_ref[...] = grad_residual + norm_backward(grad_norm * gain_mlp_ref[...], normed_in, inverse_in)
    relay(2, all_r, dp_r)
    relay(3, all_p, dp_p)
    for state in (dp_x, dp_a, dp_r, dp_p):
        finish(state)
    for copy in sends:
        copy.wait_send()


def product_kernel(x_ref, r_ref, a_ref, p_ref, grad_in_ref, grad_out_ref):
    over_rows = (((0,), (0,)), ((), ()))
    f32 = jnp.float32
    grad_out_ref[...] = lax.dot_general(a_ref[...], r_ref[...], over_rows, preferred_element_type=f32)
    grad_in_ref[...] = lax.dot_general(p_ref[...], x_ref[...], over_rows, preferred_element_type=f32)


def weight_grads(all_x, all_a, all_r, all_p):
    count, width = all_x.shape
    units = all_a.shape[1]
    step = 256
    whole = pl.BlockSpec((count, width), lambda i: (0, 0))
    part = pl.BlockSpec((count, step), lambda i: (0, i))
    made = pl.BlockSpec((step, width), lambda i: (i, 0))
    shape = jax.ShapeDtypeStruct((units, width), jnp.float32)
    grad_in, grad_out = pl.pallas_call(
        product_kernel,
        grid=(pl.cdiv(units, step),),
        in_specs=[whole, whole, part, part],
        out_specs=(made, made),
        out_shape=(shape, shape),
        compiler_params=pltpu.CompilerParams(vmem_limit_bytes=58 * 1024 * 1024),
    )(all_x, all_r, all_a, all_p)
    return grad_in.T, grad_out


def gathered_device(
    hidden_in, gain_mlp, gain_final, w_in, w_out, image_embeds, pair_ids, teacher_logits
):
    rows, width = hidden_in.shape
    units = w_in.shape[1]
    blocks, groups = lax.axis_size("blk"), lax.axis_size("dp")
    chips = groups // 2
    group = rows * blocks
    f32, bf16 = jnp.float32, jnp.bfloat16
    packed = (16 * (rows // 16), width + half_width(width))
    vmem, anywhere = pl.BlockSpec(memory_space=pltpu.VMEM), pl.BlockSpec(memory_space=pl.ANY)
    dma = pltpu.SemaphoreType.DMA
    grad_hidden, all_x, all_a, all_r, all_p = pl.pallas_call(
        functools.partial(group_kernel, blocks, chips),
        out_shape=(
            jax.ShapeDtypeStruct((rows, width), f32),
            jax.ShapeDtypeStruct((groups, group, width), bf16),
            jax.ShapeDtypeStruct((groups, group, units), bf16),
            jax.ShapeDtypeStruct((groups, group, width), bf16),
            jax.ShapeDtypeStruct((groups, group, units), bf16),
        ),
        in_specs=[vmem, vmem, vmem, anywhere, anywhere, vmem, vmem, vmem],
        out_specs=(vmem, anywhere, anywhere, anywhere, anywhere),
        scratch_shapes=[
            pltpu.VMEM((units, width), bf16),
            pltpu.VMEM(w_out.shape, bf16),
            pltpu.VMEM((blocks,) + packed, bf16),
            pltpu.VMEM((blocks,) + packed, bf16),
            pltpu.VMEM((blocks,) + packed, bf16),
            pltpu.VMEM((blocks, 8, 128), jnp.int32),
            pltpu.VMEM((blocks - 1,) + packed, bf16),
            pltpu.VMEM((blocks - 1,) + packed, bf16),
            pltpu.VMEM((blocks - 1,) + packed, bf16),
            pltpu.VMEM((blocks - 1,) + packed, bf16),
            pltpu.VMEM((group, width), f32),
            pltpu.VMEM((group, width), f32),
            pltpu.VMEM((group, width), bf16),
            pltpu.VMEM((group, width), bf16),
            pltpu.VMEM((group, width), bf16),
            pltpu.VMEM((group, units), bf16),
            pltpu.VMEM((group, units), bf16),
            pltpu.VMEM((group, units), f32),
            dma((2,)),
            dma((6, blocks - 1)),
            dma((6, blocks - 1)),
            dma((4, chips - 1)),
            dma((4, chips - 1)),
            dma((4, chips)),
            dma((4, chips)),
            dma((4,)),
        ],
        compiler_params=pltpu.CompilerParams(
            collective_id=0, has_side_effects=True, vmem_limit_bytes=58 * 1024 * 1024
        ),
    )(
        hidden_in, gain_mlp[None, :], gain_final[None, :], w_in.T, w_out, image_embeds, pair_ids[None, :],
        jnp.swapaxes(teacher_logits, 1, 2),
    )
    grad_w_in, grad_w_out = weight_grads(
        *(v.reshape(groups * group, -1) for v in (all_x, all_a, all_r, all_p))
    )
    return grad_hidden, grad_w_in, grad_w_out


def choose(*args):
    rows, width = args[0].shape
    units = args[3].shape[1]
    groups, blocks = lax.axis_size("dp"), lax.axis_size("blk")
    gathered = groups * blocks * rows * (width + units) * 2 * 2
    summed = width * units * 2 * 4
    fits = groups % 2 == 0 and groups > 2 and blocks > 1 and rows % 16 == 8 and rows > 16 and width % 128 == 0
    if fits and gathered <= summed:
        return gathered_device(*args)
    return per_device(*args)


def solution(mesh):
    in_specs = (
        P(("dp", "blk"), None),
        P(),
        P(),
        P(None, "blk"),
        P("blk", None),
        P(("dp", "blk"), None),
        P(("dp", "blk")),
        P("dp", None, "blk"),
    )
    out_specs = (P(("dp", "blk"), None), P(None, "blk"), P("blk", None))
    return jax.shard_map(
        choose, mesh=mesh, in_specs=in_specs, out_specs=out_specs, check_vma=False
    )
```

```python
import functools

import jax
import jax.numpy as jnp
from jax import lax
from jax.experimental import pallas as pl
from jax.experimental.pallas import tpu as pltpu
from jax.sharding import PartitionSpec as P

epsilon = 1e-06
logit_scale = 10.0
logit_bias = -2.0
gelu_coeff = 0.7978845608028654


def from_behind(x, axis, by):
    length = lax.axis_size(axis)
    return lax.ppermute(x, axis, [(i, (i + by) % length) for i in range(length)])


def layer_norm(values, gain_vec):
    row_mean = jnp.mean(values, axis=-1, keepdims=True)
    centred = values - row_mean
    variance = jnp.mean(centred * centred, axis=-1, keepdims=True)
    inverse = lax.rsqrt(variance + epsilon)
    normed = centred * inverse
    return (normed, inverse, normed * gain_vec)


def norm_backward(grad_normed, normed, inverse):
    mean_grad = jnp.mean(grad_normed, axis=-1, keepdims=True)
    mean_cross = jnp.mean(grad_normed * normed, axis=-1, keepdims=True)
    return inverse * (grad_normed - mean_grad - normed * mean_cross)


def gelu_both(pre_act):
    inner_arg = gelu_coeff * (pre_act + 0.044715 * pre_act * pre_act * pre_act)
    tangent = jnp.tanh(inner_arg)
    gelu_value = 0.5 * pre_act * (1.0 + tangent)
    gelu_slope = 0.5 * (1.0 + tangent) + 0.5 * pre_act * (1.0 - tangent * tangent) * gelu_coeff * (
        1.0 + 3.0 * 0.044715 * pre_act * pre_act
    )
    return (gelu_value, gelu_slope)


def tile_grad(image_rows, image_ids, text_rows, text_ids, teacher_tile):
    logits = lax.dot_general(
        image_rows, text_rows, (((1,), (1,)), ((), ())), preferred_element_type=jnp.float32
    )
    logits = logits * logit_scale + logit_bias
    same_pair = (image_ids[:, None] == text_ids[None, :]).astype(jnp.float32)
    target = 0.5 * same_pair + 0.5 * jax.nn.sigmoid(teacher_tile.astype(jnp.float32))
    pair_grad = (jax.nn.sigmoid(logits) - target).astype(jnp.bfloat16)
    return lax.dot_general(
        pair_grad, image_rows, (((0,), (0,)), ((), ())), preferred_element_type=jnp.float32
    )


def per_device(
    hidden_in, gain_mlp, gain_final, w_in, w_out, image_embeds, pair_ids, teacher_logits
):
    row_count = hidden_in.shape[0]
    width = hidden_in.shape[1]
    blocks = lax.axis_size("blk")
    own_index = lax.axis_index("blk")
    hidden = hidden_in.astype(jnp.float32)
    normed_in, inverse_in, scaled_in = layer_norm(hidden, gain_mlp)
    mlp_input = scaled_in.astype(jnp.bfloat16)
    group_input = lax.all_gather(mlp_input, "blk", axis=0, tiled=True)
    pre_act = jnp.dot(group_input, w_in, preferred_element_type=jnp.float32)
    gelu_value, gelu_slope = gelu_both(pre_act)
    activation = gelu_value.astype(jnp.bfloat16)
    piece = activation
    residual = hidden + lax.psum_scatter(
        jnp.dot(piece, w_out, preferred_element_type=jnp.float32),
        "blk",
        scatter_dimension=0,
        tiled=True,
    )
    normed_out, inverse_out, final_out = layer_norm(residual, gain_final)
    length = jnp.sqrt(jnp.sum(final_out * final_out, axis=-1, keepdims=True) + epsilon)
    unit_text = final_out / length
    text_embed = unit_text.astype(jnp.bfloat16)
    image_float = image_embeds.astype(jnp.float32)
    image_unit = (
        image_float
        * lax.rsqrt(jnp.sum(image_float * image_float, axis=-1, keepdims=True) + epsilon)
    ).astype(jnp.bfloat16)
    group_ids = lax.all_gather(pair_ids, "blk", axis=0, tiled=True)
    teacher_cols = teacher_logits[0]
    empty_grads = jnp.zeros((row_count, width), jnp.float32)

    def rotate_once(turn_index, loop_state):
        image_rows, text_grads = loop_state
        source = (own_index - turn_index + blocks) % blocks
        image_ids = lax.dynamic_slice_in_dim(group_ids, source * row_count, row_count, 0)
        teacher_tile = lax.dynamic_slice_in_dim(teacher_cols, source * row_count, row_count, 0)
        text_grads = text_grads + tile_grad(
            image_rows, image_ids, text_embed, pair_ids, teacher_tile
        )
        image_rows = from_behind(image_rows, "blk", 1)
        return (image_rows, text_grads)

    loop_state = lax.fori_loop(0, blocks, rotate_once, (image_unit, empty_grads))
    text_grad = logit_scale * loop_state[1]
    radial = jnp.sum(unit_text * text_grad, axis=-1, keepdims=True)
    grad_final = (text_grad - unit_text * radial) / length
    grad_residual = norm_backward(grad_final * gain_final, normed_out, inverse_out)
    residual_rows = grad_residual.astype(jnp.bfloat16)
    group_grads = lax.all_gather(residual_rows, "blk", axis=0, tiled=True)
    grad_activation = lax.dot_general(
        group_grads, w_out, (((1,), (1,)), ((), ())), preferred_element_type=jnp.float32
    )
    grad_pre = (grad_activation * gelu_slope).astype(jnp.bfloat16)
    part_w_out = lax.dot_general(
        activation, group_grads, (((0,), (0,)), ((), ())), preferred_element_type=jnp.float32
    )
    part_w_in = lax.dot_general(
        group_input, grad_pre, (((0,), (0,)), ((), ())), preferred_element_type=jnp.float32
    )
    piece = grad_pre
    grad_input_norm = lax.psum_scatter(
        lax.dot_general(piece, w_in, (((1,), (1,)), ((), ())), preferred_element_type=jnp.float32),
        "blk",
        scatter_dimension=0,
        tiled=True,
    )
    grad_w_in, grad_w_out = lax.psum((part_w_in, part_w_out), "dp")
    grad_hidden = grad_residual + norm_backward(grad_input_norm * gain_mlp, normed_in, inverse_in)
    return (grad_hidden, grad_w_in, grad_w_out)


def half_width(width):
    return -(-width // 256) * 128


def pack(rows):
    width = rows.shape[1]
    half = half_width(width)
    low, high = rows[-8:, :half], rows[-8:, half:]
    if width - half < half:
        high = jnp.concatenate([high, jnp.zeros((8, 2 * half - width), rows.dtype)], axis=1)
    side = jnp.concatenate([low, high], axis=0)
    if rows.shape[0] > 24:
        side = jnp.concatenate([side, jnp.zeros((rows.shape[0] - 24, half), rows.dtype)], axis=0)
    return jnp.concatenate([rows[:-8], side], axis=1).astype(jnp.bfloat16)


def unpack(slab, width):
    half = half_width(width)
    slab = slab.astype(jnp.float32)
    last = jnp.concatenate([slab[:8, width:], slab[8:16, width : 2 * width - half]], axis=1)
    return jnp.concatenate([slab[:, :width], last], axis=0)


def tiles_of(extent, size):
    return [(at, min(size, extent - at)) for at in range(0, extent, size)]


def group_kernel(
    blocks, chips,
    hidden_ref, gain_mlp_ref, gain_final_ref, w_in_hbm, w_out_hbm, image_ref, ids_ref, teacher_ref,
    grad_hidden_ref, all_x, all_r,
    w_in, w_out, slab_x, slab_i, slab_r, id_rows, out_1, in_1, out_2, in_2, partial,
    rows_f32, group_x, group_i, group_r, group_a, group_p, slope,
    load_sem, blk_send, blk_recv, chip_send, chip_recv, core_send, core_recv, own_sem,
):
    f32, bf16 = jnp.float32, jnp.bfloat16
    rows, width = hidden_ref.shape
    hidden_units = w_in.shape[0]
    last_dims = (((1,), (1,)), ((), ()))
    dp, blk = lax.axis_index("dp"), lax.axis_index("blk")
    chip, core = dp // 2, dp % 2
    tile = 384

    loads = [
        pltpu.make_async_copy(w_in_hbm, w_in, load_sem.at[0]),
        pltpu.make_async_copy(w_out_hbm, w_out, load_sem.at[1]),
    ]
    for load in loads:
        load.start()

    def blk_peer(k):
        return lax.rem(blk + k, blocks)

    def chip_peer(k):
        return lax.rem(chip + k, chips) * 2 + core

    barrier = pltpu.get_barrier_semaphore()
    for k in range(1, blocks):
        pl.semaphore_signal(barrier, inc=1, device_id={"dp": dp, "blk": blk_peer(k)})
    for k in range(1, chips):
        pl.semaphore_signal(barrier, inc=1, device_id={"dp": chip_peer(k), "blk": blk})
    pl.semaphore_signal(barrier, inc=1, device_id={"dp": chip * 2 + 1 - core, "blk": blk})

    sends = []

    def blk_copy(phase, k, src, dst):
        return pltpu.make_async_remote_copy(
            src_ref=src, dst_ref=dst, send_sem=blk_send.at[phase, k - 1], recv_sem=blk_recv.at[phase, k - 1],
            device_id={"dp": dp, "blk": blk_peer(k)},
        )

    def share(phase, buffer):
        copies = [blk_copy(phase, k, buffer.at[blk], buffer.at[blk]) for k in range(1, blocks)]
        for copy in copies:
            copy.start()
        sends.extend(copies)
        return copies

    def arrived(copies):
        for copy in copies:
            copy.wait_recv()

    def spread(kind, source, landing):
        copies = []
        for k in range(1, chips):
            copies.append(pltpu.make_async_remote_copy(
                src_ref=source, dst_ref=landing.at[dp], send_sem=chip_send.at[kind, k - 1],
                recv_sem=chip_recv.at[kind, k - 1], device_id={"dp": chip_peer(k), "blk": blk},
            ))
        other = pltpu.make_async_remote_copy(
            src_ref=source, dst_ref=landing.at[dp], send_sem=core_send.at[kind, 0],
            recv_sem=core_recv.at[kind, 0], device_id={"dp": chip * 2 + 1 - core, "blk": blk},
        )
        own = pltpu.make_async_copy(source, landing.at[dp], own_sem.at[kind])
        for copy in copies + [other, own]:
            copy.start()
        sends.extend(copies + [other])
        return copies, [other], own

    def relay(kind, landing, state):
        copies, others, own = state
        for k in range(1, chips):
            copies[k - 1].wait_recv()
            place = landing.at[lax.rem(chip + chips - k, chips) * 2 + core]
            other = pltpu.make_async_remote_copy(
                src_ref=place, dst_ref=place, send_sem=core_send.at[kind, k],
                recv_sem=core_recv.at[kind, k], device_id={"dp": chip * 2 + 1 - core, "blk": blk},
            )
            other.start()
            others.append(other)
            sends.append(other)

    def finish(state):
        arrived(state[1])
        state[2].wait()

    def regroup(buffer, target):
        for j in range(blocks):
            rows_f32[j * rows : (j + 1) * rows, :] = unpack(buffer[j], width)
        for at, size in tiles_of(width, tile):
            target[:, at : at + size] = rows_f32[:, at : at + size].astype(bf16)

    def scatter(phase, out_buf, in_buf):
        for k in range(1, blocks):
            out_buf[k - 1] = pack(partial[pl.ds(pl.multiple_of(blk_peer(k) * rows, 8), rows), :])
        copies = [blk_copy(phase, k, out_buf.at[k - 1], in_buf.at[k - 1]) for k in range(1, blocks)]
        for copy in copies:
            copy.start()
        sends.extend(copies)
        return copies

    def collect(copies, in_buf):
        total = partial[pl.ds(pl.multiple_of(blk * rows, 8), rows), :]
        for k in range(1, blocks):
            copies[k - 1].wait_recv()
            total = total + unpack(in_buf[k - 1], width)
        return total

    hidden = hidden_ref[...].astype(f32)
    normed_in, inverse_in, scaled_in = layer_norm(hidden, gain_mlp_ref[...][None, :])
    slab_x[blk] = pack(scaled_in.astype(bf16).astype(f32))
    pl.semaphore_wait(barrier, blocks - 1 + chips - 1 + 1)
    came_x = share(0, slab_x)

    image = image_ref[...].astype(f32)
    image = image * lax.rsqrt(jnp.sum(image * image, axis=-1, keepdims=True) + epsilon)
    slab_i[blk] = pack(image.astype(bf16).astype(f32))
    square = (rows, rows)
    diagonal = lax.broadcasted_iota(jnp.int32, square, 0) == lax.broadcasted_iota(jnp.int32, square, 1)
    own_ids = ids_ref[...]
    column = jnp.sum(jnp.where(diagonal, own_ids, 0), axis=1, keepdims=True)
    id_rows[blk] = jnp.broadcast_to(jnp.concatenate([own_ids, jnp.zeros((1, 128 - rows), jnp.int32)], axis=1), id_rows.shape[1:])

    arrived(came_x)
    came_i = share(1, slab_i)
    came_ids = share(2, id_rows)
    regroup(slab_x, group_x)
    dp_x = spread(0, group_x, all_x)
    loads[0].wait()
    for at, size in tiles_of(hidden_units, tile):
        pre_act = lax.dot_general(
            group_x[...], w_in[at : at + size, :], last_dims, preferred_element_type=f32
        )
        value, steep = gelu_both(pre_act)
        group_a[:, at : at + size] = value.astype(bf16)
        slope[:, at : at + size] = steep
    loads[1].wait()
    for at, size in tiles_of(width, tile):
        partial[:, at : at + size] = jnp.dot(group_a[...], w_out[:, at : at + size], preferred_element_type=f32)
    sums_1 = scatter(3, out_1, in_1)

    arrived(came_i)
    arrived(came_ids)
    regroup(slab_i, group_i)
    teacher = jax.nn.sigmoid(teacher_ref[0].astype(f32))
    image_ids = jnp.concatenate([id_rows[j][:1, :rows] for j in range(blocks)], axis=1)
    same_pair = (image_ids == column).astype(f32)
    target = 0.5 * same_pair + 0.5 * teacher

    residual = hidden + collect(sums_1, in_1)
    normed_out, inverse_out, final_out = layer_norm(residual, gain_final_ref[...][None, :])
    length = jnp.sqrt(jnp.sum(final_out * final_out, axis=-1, keepdims=True) + epsilon)
    unit_text = final_out / length
    logits = lax.dot_general(unit_text.astype(bf16), group_i[...], last_dims, preferred_element_type=f32)
    logits = logits * logit_scale + logit_bias
    pair_grad = (jax.nn.sigmoid(logits) - target).astype(bf16)
    text_grad = logit_scale * jnp.dot(pair_grad, group_i[...], preferred_element_type=f32)
    radial = jnp.sum(unit_text * text_grad, axis=-1, keepdims=True)
    grad_final = (text_grad - unit_text * radial) / length
    grad_residual = norm_backward(grad_final * gain_final_ref[...][None, :], normed_out, inverse_out)
    slab_r[blk] = pack(grad_residual.astype(bf16).astype(f32))
    came_r = share(4, slab_r)
    relay(0, all_x, dp_x)
    arrived(came_r)
    regroup(slab_r, group_r)
    dp_r = spread(1, group_r, all_r)
    for at, size in tiles_of(hidden_units, tile):
        grad_act = lax.dot_general(group_r[...], w_out[at : at + size, :], last_dims, preferred_element_type=f32)
        group_p[:, at : at + size] = (grad_act * slope[:, at : at + size]).astype(bf16)
    for at, size in tiles_of(width, tile):
        partial[:, at : at + size] = jnp.dot(group_p[...], w_in[:, at : at + size], preferred_element_type=f32)
    sums_2 = scatter(5, out_2, in_2)
    grad_norm = collect(sums_2, in_2)
    grad_hidden_ref[...] = grad_residual + norm_backward(grad_norm * gain_mlp_ref[...][None, :], normed_in, inverse_in)
    relay(1, all_r, dp_r)
    for state in (dp_x, dp_r):
        finish(state)
    for copy in sends:
        copy.wait_send()


def product_kernel(x_ref, r_ref, w_in_ref, w_out_ref, grad_in_ref, grad_out_ref):
    f32, bf16 = jnp.float32, jnp.bfloat16
    last_dims = (((1,), (1,)), ((), ()))
    pre_act = lax.dot_general(w_in_ref[...], x_ref[...], last_dims, preferred_element_type=f32)
    value, steep = gelu_both(pre_act)
    grad_act = lax.dot_general(w_out_ref[...], r_ref[...], last_dims, preferred_element_type=f32)
    grad_out_ref[...] = jnp.dot(value.astype(bf16), r_ref[...], preferred_element_type=f32)
    grad_in_ref[...] = jnp.dot((grad_act * steep).astype(bf16), x_ref[...], preferred_element_type=f32)


def weight_grads(all_x, all_r, w_in, w_out):
    count, width = all_x.shape
    units = w_in.shape[0]
    step = -(-units // 64) * 16
    whole = pl.BlockSpec((count, width), lambda i: (0, 0))
    part = pl.BlockSpec((step, width), lambda i: (i, 0))
    shape = jax.ShapeDtypeStruct((units, width), jnp.float32)
    grad_in, grad_out = pl.pallas_call(
        product_kernel,
        grid=(pl.cdiv(units, step),),
        in_specs=[whole, whole, part, part],
        out_specs=(part, part),
        out_shape=(shape, shape),
        compiler_params=pltpu.CompilerParams(vmem_limit_bytes=58 * 1024 * 1024),
    )(all_x, all_r, w_in, w_out)
    return grad_in.T, grad_out


def gathered_device(
    hidden_in, gain_mlp, gain_final, w_in, w_out, image_embeds, pair_ids, teacher_logits
):
    rows, width = hidden_in.shape
    units = w_in.shape[1]
    blocks, groups = lax.axis_size("blk"), lax.axis_size("dp")
    chips = groups // 2
    group = rows * blocks
    f32, bf16 = jnp.float32, jnp.bfloat16
    packed = (16 * (rows // 16), width + half_width(width))
    vmem, anywhere = pl.BlockSpec(memory_space=pltpu.VMEM), pl.BlockSpec(memory_space=pl.ANY)
    dma = pltpu.SemaphoreType.DMA
    grad_hidden, all_x, all_r = pl.pallas_call(
        functools.partial(group_kernel, blocks, chips),
        out_shape=(
            jax.ShapeDtypeStruct((rows, width), f32),
            jax.ShapeDtypeStruct((groups, group, width), bf16),
            jax.ShapeDtypeStruct((groups, group, width), bf16),
        ),
        in_specs=[vmem, vmem, vmem, anywhere, anywhere, vmem, vmem, vmem],
        out_specs=(vmem, anywhere, anywhere),
        scratch_shapes=[
            pltpu.VMEM((units, width), bf16),
            pltpu.VMEM(w_out.shape, bf16),
            pltpu.VMEM((blocks,) + packed, bf16),
            pltpu.VMEM((blocks,) + packed, bf16),
            pltpu.VMEM((blocks,) + packed, bf16),
            pltpu.VMEM((blocks, 8, 128), jnp.int32),
            pltpu.VMEM((blocks - 1,) + packed, bf16),
            pltpu.VMEM((blocks - 1,) + packed, bf16),
            pltpu.VMEM((blocks - 1,) + packed, bf16),
            pltpu.VMEM((blocks - 1,) + packed, bf16),
            pltpu.VMEM((group, width), f32),
            pltpu.VMEM((group, width), f32),
            pltpu.VMEM((group, width), bf16),
            pltpu.VMEM((group, width), bf16),
            pltpu.VMEM((group, width), bf16),
            pltpu.VMEM((group, units), bf16),
            pltpu.VMEM((group, units), bf16),
            pltpu.VMEM((group, units), f32),
            dma((2,)),
            dma((6, blocks - 1)),
            dma((6, blocks - 1)),
            dma((2, chips - 1)),
            dma((2, chips - 1)),
            dma((2, chips)),
            dma((2, chips)),
            dma((2,)),
        ],
        compiler_params=pltpu.CompilerParams(
            collective_id=0, has_side_effects=True, vmem_limit_bytes=58 * 1024 * 1024
        ),
    )(
        hidden_in, gain_mlp, gain_final, w_in.T, w_out, image_embeds, pair_ids[None, :],
        jnp.swapaxes(teacher_logits, 1, 2),
    )
    grad_w_in, grad_w_out = weight_grads(
        all_x.reshape(groups * group, width), all_r.reshape(groups * group, width), w_in.T, w_out
    )
    return grad_hidden, grad_w_in, grad_w_out


def choose(*args):
    rows, width = args[0].shape
    units = args[3].shape[1]
    groups, blocks = lax.axis_size("dp"), lax.axis_size("blk")
    gathered = groups * blocks * rows * width * 2 * 2
    summed = width * units * 2 * 4
    fits = groups % 2 == 0 and groups > 2 and blocks > 1 and rows % 16 == 8 and rows > 16 and width % 128 == 0
    if fits and gathered <= summed:
        return gathered_device(*args)
    return per_device(*args)


def solution(mesh):
    in_specs = (
        P(("dp", "blk"), None),
        P(),
        P(),
        P(None, "blk"),
        P("blk", None),
        P(("dp", "blk"), None),
        P(("dp", "blk")),
        P("dp", None, "blk"),
    )
    out_specs = (P(("dp", "blk"), None), P(None, "blk"), P("blk", None))
    return jax.shard_map(
        choose, mesh=mesh, in_specs=in_specs, out_specs=out_specs, check_vma=False
    )
```

```python
import functools

import jax
import jax.numpy as jnp
from jax import lax
from jax.experimental import pallas as pl
from jax.experimental.pallas import tpu as pltpu
from jax.sharding import PartitionSpec as P

epsilon = 1e-06
logit_scale = 10.0
logit_bias = -2.0
gelu_coeff = 0.7978845608028654


def from_behind(x, axis, by):
    length = lax.axis_size(axis)
    return lax.ppermute(x, axis, [(i, (i + by) % length) for i in range(length)])


def layer_norm(values, gain_vec):
    row_mean = jnp.mean(values, axis=-1, keepdims=True)
    centred = values - row_mean
    variance = jnp.mean(centred * centred, axis=-1, keepdims=True)
    inverse = lax.rsqrt(variance + epsilon)
    normed = centred * inverse
    return (normed, inverse, normed * gain_vec)


def norm_backward(grad_normed, normed, inverse):
    mean_grad = jnp.mean(grad_normed, axis=-1, keepdims=True)
    mean_cross = jnp.mean(grad_normed * normed, axis=-1, keepdims=True)
    return inverse * (grad_normed - mean_grad - normed * mean_cross)


def gelu_both(pre_act):
    inner_arg = gelu_coeff * (pre_act + 0.044715 * pre_act * pre_act * pre_act)
    tangent = jnp.tanh(inner_arg)
    gelu_value = 0.5 * pre_act * (1.0 + tangent)
    gelu_slope = 0.5 * (1.0 + tangent) + 0.5 * pre_act * (1.0 - tangent * tangent) * gelu_coeff * (
        1.0 + 3.0 * 0.044715 * pre_act * pre_act
    )
    return (gelu_value, gelu_slope)


def tile_grad(image_rows, image_ids, text_rows, text_ids, teacher_tile):
    logits = lax.dot_general(
        image_rows, text_rows, (((1,), (1,)), ((), ())), preferred_element_type=jnp.float32
    )
    logits = logits * logit_scale + logit_bias
    same_pair = (image_ids[:, None] == text_ids[None, :]).astype(jnp.float32)
    target = 0.5 * same_pair + 0.5 * jax.nn.sigmoid(teacher_tile.astype(jnp.float32))
    pair_grad = (jax.nn.sigmoid(logits) - target).astype(jnp.bfloat16)
    return lax.dot_general(
        pair_grad, image_rows, (((0,), (0,)), ((), ())), preferred_element_type=jnp.float32
    )


def per_device(
    hidden_in, gain_mlp, gain_final, w_in, w_out, image_embeds, pair_ids, teacher_logits
):
    row_count = hidden_in.shape[0]
    width = hidden_in.shape[1]
    blocks = lax.axis_size("blk")
    own_index = lax.axis_index("blk")
    hidden = hidden_in.astype(jnp.float32)
    normed_in, inverse_in, scaled_in = layer_norm(hidden, gain_mlp)
    mlp_input = scaled_in.astype(jnp.bfloat16)
    group_input = lax.all_gather(mlp_input, "blk", axis=0, tiled=True)
    pre_act = jnp.dot(group_input, w_in, preferred_element_type=jnp.float32)
    gelu_value, gelu_slope = gelu_both(pre_act)
    activation = gelu_value.astype(jnp.bfloat16)
    piece = activation
    residual = hidden + lax.psum_scatter(
        jnp.dot(piece, w_out, preferred_element_type=jnp.float32),
        "blk",
        scatter_dimension=0,
        tiled=True,
    )
    normed_out, inverse_out, final_out = layer_norm(residual, gain_final)
    length = jnp.sqrt(jnp.sum(final_out * final_out, axis=-1, keepdims=True) + epsilon)
    unit_text = final_out / length
    text_embed = unit_text.astype(jnp.bfloat16)
    image_float = image_embeds.astype(jnp.float32)
    image_unit = (
        image_float
        * lax.rsqrt(jnp.sum(image_float * image_float, axis=-1, keepdims=True) + epsilon)
    ).astype(jnp.bfloat16)
    group_ids = lax.all_gather(pair_ids, "blk", axis=0, tiled=True)
    teacher_cols = teacher_logits[0]
    empty_grads = jnp.zeros((row_count, width), jnp.float32)

    def rotate_once(turn_index, loop_state):
        image_rows, text_grads = loop_state
        source = (own_index - turn_index + blocks) % blocks
        image_ids = lax.dynamic_slice_in_dim(group_ids, source * row_count, row_count, 0)
        teacher_tile = lax.dynamic_slice_in_dim(teacher_cols, source * row_count, row_count, 0)
        text_grads = text_grads + tile_grad(
            image_rows, image_ids, text_embed, pair_ids, teacher_tile
        )
        image_rows = from_behind(image_rows, "blk", 1)
        return (image_rows, text_grads)

    loop_state = lax.fori_loop(0, blocks, rotate_once, (image_unit, empty_grads))
    text_grad = logit_scale * loop_state[1]
    radial = jnp.sum(unit_text * text_grad, axis=-1, keepdims=True)
    grad_final = (text_grad - unit_text * radial) / length
    grad_residual = norm_backward(grad_final * gain_final, normed_out, inverse_out)
    residual_rows = grad_residual.astype(jnp.bfloat16)
    group_grads = lax.all_gather(residual_rows, "blk", axis=0, tiled=True)
    grad_activation = lax.dot_general(
        group_grads, w_out, (((1,), (1,)), ((), ())), preferred_element_type=jnp.float32
    )
    grad_pre = (grad_activation * gelu_slope).astype(jnp.bfloat16)
    part_w_out = lax.dot_general(
        activation, group_grads, (((0,), (0,)), ((), ())), preferred_element_type=jnp.float32
    )
    part_w_in = lax.dot_general(
        group_input, grad_pre, (((0,), (0,)), ((), ())), preferred_element_type=jnp.float32
    )
    piece = grad_pre
    grad_input_norm = lax.psum_scatter(
        lax.dot_general(piece, w_in, (((1,), (1,)), ((), ())), preferred_element_type=jnp.float32),
        "blk",
        scatter_dimension=0,
        tiled=True,
    )
    grad_w_in, grad_w_out = lax.psum((part_w_in, part_w_out), "dp")
    grad_hidden = grad_residual + norm_backward(grad_input_norm * gain_mlp, normed_in, inverse_in)
    return (grad_hidden, grad_w_in, grad_w_out)


def half_width(width):
    return -(-width // 256) * 128


def pack(rows):
    width = rows.shape[1]
    half = half_width(width)
    low, high = rows[-8:, :half], rows[-8:, half:]
    if width - half < half:
        high = jnp.concatenate([high, jnp.zeros((8, 2 * half - width), rows.dtype)], axis=1)
    side = jnp.concatenate([low, high], axis=0)
    if rows.shape[0] > 24:
        side = jnp.concatenate([side, jnp.zeros((rows.shape[0] - 24, half), rows.dtype)], axis=0)
    return jnp.concatenate([rows[:-8], side], axis=1).astype(jnp.bfloat16)


def unpack(slab, width):
    half = half_width(width)
    slab = slab.astype(jnp.float32)
    last = jnp.concatenate([slab[:8, width:], slab[8:16, width : 2 * width - half]], axis=1)
    return jnp.concatenate([slab[:, :width], last], axis=0)


def tiles_of(extent, size):
    return [(at, min(size, extent - at)) for at in range(0, extent, size)]


def group_kernel(
    blocks, chips,
    hidden_ref, gain_mlp_ref, gain_final_ref, w_in_hbm, w_out_hbm, image_ref, ids_ref, teacher_ref,
    grad_hidden_ref, all_x, all_r, act_hbm, steep_hbm,
    w_in, w_out, slab_x, slab_i, slab_r, id_rows, out_1, in_1, out_2, in_2, partial,
    rows_f32, group_x, group_i, group_r, group_a, group_p, slope, x_rows, act_all, steep_all, late_sem,
    load_sem, blk_send, blk_recv, chip_send, chip_recv, core_send, core_recv, own_sem,
):
    f32, bf16 = jnp.float32, jnp.bfloat16
    rows, width = hidden_ref.shape
    hidden_units = w_in.shape[0]
    last_dims = (((1,), (1,)), ((), ()))
    dp, blk = lax.axis_index("dp"), lax.axis_index("blk")
    chip, core = dp // 2, dp % 2
    tile = 384

    loads = [
        pltpu.make_async_copy(w_in_hbm, w_in, load_sem.at[0]),
        pltpu.make_async_copy(w_out_hbm, w_out, load_sem.at[1]),
    ]
    for load in loads:
        load.start()

    def blk_peer(k):
        return lax.rem(blk + k, blocks)

    def chip_peer(k):
        return lax.rem(chip + k, chips) * 2 + core

    barrier = pltpu.get_barrier_semaphore()
    for k in range(1, blocks):
        pl.semaphore_signal(barrier, inc=1, device_id={"dp": dp, "blk": blk_peer(k)})
    for k in range(1, chips):
        pl.semaphore_signal(barrier, inc=1, device_id={"dp": chip_peer(k), "blk": blk})
    pl.semaphore_signal(barrier, inc=1, device_id={"dp": chip * 2 + 1 - core, "blk": blk})

    sends = []

    def blk_copy(phase, k, src, dst):
        return pltpu.make_async_remote_copy(
            src_ref=src, dst_ref=dst, send_sem=blk_send.at[phase, k - 1], recv_sem=blk_recv.at[phase, k - 1],
            device_id={"dp": dp, "blk": blk_peer(k)},
        )

    def share(phase, buffer):
        copies = [blk_copy(phase, k, buffer.at[blk], buffer.at[blk]) for k in range(1, blocks)]
        for copy in copies:
            copy.start()
        sends.extend(copies)
        return copies

    def arrived(copies):
        for copy in copies:
            copy.wait_recv()

    def spread(kind, source, landing):
        copies = []
        for k in range(1, chips):
            copies.append(pltpu.make_async_remote_copy(
                src_ref=source, dst_ref=landing.at[dp], send_sem=chip_send.at[kind, k - 1],
                recv_sem=chip_recv.at[kind, k - 1], device_id={"dp": chip_peer(k), "blk": blk},
            ))
        other = pltpu.make_async_remote_copy(
            src_ref=source, dst_ref=landing.at[dp], send_sem=core_send.at[kind, 0],
            recv_sem=core_recv.at[kind, 0], device_id={"dp": chip * 2 + 1 - core, "blk": blk},
        )
        own = pltpu.make_async_copy(source, landing.at[dp], own_sem.at[kind])
        for copy in copies + [other, own]:
            copy.start()
        sends.extend(copies + [other])
        return copies, [other], own

    def relay(kind, landing, state):
        copies, others, own = state
        for k in range(1, chips):
            copies[k - 1].wait_recv()
            place = landing.at[lax.rem(chip + chips - k, chips) * 2 + core]
            other = pltpu.make_async_remote_copy(
                src_ref=place, dst_ref=place, send_sem=core_send.at[kind, k],
                recv_sem=core_recv.at[kind, k], device_id={"dp": chip * 2 + 1 - core, "blk": blk},
            )
            other.start()
            others.append(other)
            sends.append(other)

    def finish(state):
        arrived(state[1])
        state[2].wait()

    def regroup(buffer, target):
        for j in range(blocks):
            rows_f32[j * rows : (j + 1) * rows, :] = unpack(buffer[j], width)
        for at, size in tiles_of(width, tile):
            target[:, at : at + size] = rows_f32[:, at : at + size].astype(bf16)

    def scatter(phase, out_buf, in_buf):
        for k in range(1, blocks):
            out_buf[k - 1] = pack(partial[pl.ds(pl.multiple_of(blk_peer(k) * rows, 8), rows), :])
        copies = [blk_copy(phase, k, out_buf.at[k - 1], in_buf.at[k - 1]) for k in range(1, blocks)]
        for copy in copies:
            copy.start()
        sends.extend(copies)
        return copies

    def collect(copies, in_buf):
        total = partial[pl.ds(pl.multiple_of(blk * rows, 8), rows), :]
        for k in range(1, blocks):
            copies[k - 1].wait_recv()
            total = total + unpack(in_buf[k - 1], width)
        return total

    hidden = hidden_ref[...].astype(f32)
    normed_in, inverse_in, scaled_in = layer_norm(hidden, gain_mlp_ref[...][None, :])
    slab_x[blk] = pack(scaled_in.astype(bf16).astype(f32))
    pl.semaphore_wait(barrier, blocks - 1 + chips - 1 + 1)
    came_x = share(0, slab_x)

    image = image_ref[...].astype(f32)
    image = image * lax.rsqrt(jnp.sum(image * image, axis=-1, keepdims=True) + epsilon)
    slab_i[blk] = pack(image.astype(bf16).astype(f32))
    square = (rows, rows)
    diagonal = lax.broadcasted_iota(jnp.int32, square, 0) == lax.broadcasted_iota(jnp.int32, square, 1)
    own_ids = ids_ref[...]
    column = jnp.sum(jnp.where(diagonal, own_ids, 0), axis=1, keepdims=True)
    id_rows[blk] = jnp.broadcast_to(jnp.concatenate([own_ids, jnp.zeros((1, 128 - rows), jnp.int32)], axis=1), id_rows.shape[1:])

    arrived(came_x)
    came_i = share(1, slab_i)
    came_ids = share(2, id_rows)
    regroup(slab_x, group_x)
    dp_x = spread(0, group_x, all_x)
    loads[0].wait()
    for at, size in tiles_of(hidden_units, tile):
        pre_act = lax.dot_general(
            group_x[...], w_in[at : at + size, :], last_dims, preferred_element_type=f32
        )
        value, steep = gelu_both(pre_act)
        group_a[:, at : at + size] = value.astype(bf16)
        slope[:, at : at + size] = steep
    loads[1].wait()
    for at, size in tiles_of(width, tile):
        partial[:, at : at + size] = jnp.dot(group_a[...], w_out[:, at : at + size], preferred_element_type=f32)
    sums_1 = scatter(3, out_1, in_1)

    arrived(came_i)
    arrived(came_ids)
    regroup(slab_i, group_i)
    teacher = jax.nn.sigmoid(teacher_ref[0].astype(f32))
    image_ids = jnp.concatenate([id_rows[j][:1, :rows] for j in range(blocks)], axis=1)
    same_pair = (image_ids == column).astype(f32)
    target = 0.5 * same_pair + 0.5 * teacher

    residual = hidden + collect(sums_1, in_1)
    normed_out, inverse_out, final_out = layer_norm(residual, gain_final_ref[...][None, :])
    length = jnp.sqrt(jnp.sum(final_out * final_out, axis=-1, keepdims=True) + epsilon)
    unit_text = final_out / length
    logits = lax.dot_general(unit_text.astype(bf16), group_i[...], last_dims, preferred_element_type=f32)
    logits = logits * logit_scale + logit_bias
    pair_grad = (jax.nn.sigmoid(logits) - target).astype(bf16)
    text_grad = logit_scale * jnp.dot(pair_grad, group_i[...], preferred_element_type=f32)
    radial = jnp.sum(unit_text * text_grad, axis=-1, keepdims=True)
    grad_final = (text_grad - unit_text * radial) / length
    grad_residual = norm_backward(grad_final * gain_final_ref[...][None, :], normed_out, inverse_out)
    slab_r[blk] = pack(grad_residual.astype(bf16).astype(f32))
    came_r = share(4, slab_r)
    relay(0, all_x, dp_x)
    arrived(came_r)
    regroup(slab_r, group_r)
    dp_r = spread(1, group_r, all_r)
    for at, size in tiles_of(hidden_units, tile):
        grad_act = lax.dot_general(group_r[...], w_out[at : at + size, :], last_dims, preferred_element_type=f32)
        group_p[:, at : at + size] = (grad_act * slope[:, at : at + size]).astype(bf16)
    for at, size in tiles_of(width, tile):
        partial[:, at : at + size] = jnp.dot(group_p[...], w_in[:, at : at + size], preferred_element_type=f32)
    sums_2 = scatter(5, out_2, in_2)
    finish(dp_x)
    fetch = pltpu.make_async_copy(all_x, x_rows, late_sem.at[0])
    fetch.start()
    fetch.wait()
    count = x_rows.shape[0] * x_rows.shape[1]
    for at, size in tiles_of(hidden_units, -(-hidden_units // 64) * 16):
        pre_act = lax.dot_general(
            w_in[at : at + size, :], x_rows[...].reshape(count, width), last_dims, preferred_element_type=f32
        )
        value, steep = gelu_both(pre_act)
        act_all[at : at + size, :] = value.astype(bf16)
        steep_all[at : at + size, :] = steep
    stores = [
        pltpu.make_async_copy(act_all, act_hbm, late_sem.at[1]),
        pltpu.make_async_copy(steep_all, steep_hbm, late_sem.at[2]),
    ]
    for store in stores:
        store.start()
    grad_norm = collect(sums_2, in_2)
    grad_hidden_ref[...] = grad_residual + norm_backward(grad_norm * gain_mlp_ref[...][None, :], normed_in, inverse_in)
    relay(1, all_r, dp_r)
    finish(dp_r)
    for store in stores:
        store.wait()
    for copy in sends:
        copy.wait_send()


def product_kernel(x_ref, r_ref, act_ref, steep_ref, w_out_ref, grad_in_ref, grad_out_ref):
    f32, bf16 = jnp.float32, jnp.bfloat16
    last_dims = (((1,), (1,)), ((), ()))
    grad_act = lax.dot_general(w_out_ref[...], r_ref[...], last_dims, preferred_element_type=f32)
    grad_out_ref[...] = jnp.dot(act_ref[...], r_ref[...], preferred_element_type=f32)
    grad_in_ref[...] = jnp.dot((grad_act * steep_ref[...]).astype(bf16), x_ref[...], preferred_element_type=f32)


def weight_grads(all_x, all_r, act_all, steep_all, w_out):
    count, width = all_x.shape
    units = w_out.shape[0]
    step = -(-units // 64) * 16
    whole = pl.BlockSpec((count, width), lambda i: (0, 0))
    part = pl.BlockSpec((step, width), lambda i: (i, 0))
    turned = pl.BlockSpec((step, count), lambda i: (i, 0))
    shape = jax.ShapeDtypeStruct((units, width), jnp.float32)
    grad_in, grad_out = pl.pallas_call(
        product_kernel,
        grid=(pl.cdiv(units, step),),
        in_specs=[whole, whole, turned, turned, part],
        out_specs=(part, part),
        out_shape=(shape, shape),
        compiler_params=pltpu.CompilerParams(vmem_limit_bytes=58 * 1024 * 1024),
    )(all_x, all_r, act_all, steep_all, w_out)
    return grad_in.T, grad_out


def gathered_device(
    hidden_in, gain_mlp, gain_final, w_in, w_out, image_embeds, pair_ids, teacher_logits
):
    rows, width = hidden_in.shape
    units = w_in.shape[1]
    blocks, groups = lax.axis_size("blk"), lax.axis_size("dp")
    chips = groups // 2
    group = rows * blocks
    f32, bf16 = jnp.float32, jnp.bfloat16
    packed = (16 * (rows // 16), width + half_width(width))
    vmem, anywhere = pl.BlockSpec(memory_space=pltpu.VMEM), pl.BlockSpec(memory_space=pl.ANY)
    dma = pltpu.SemaphoreType.DMA
    grad_hidden, all_x, all_r, act_all, steep_all = pl.pallas_call(
        functools.partial(group_kernel, blocks, chips),
        out_shape=(
            jax.ShapeDtypeStruct((rows, width), f32),
            jax.ShapeDtypeStruct((groups, group, width), bf16),
            jax.ShapeDtypeStruct((groups, group, width), bf16),
            jax.ShapeDtypeStruct((units, groups * group), bf16),
            jax.ShapeDtypeStruct((units, groups * group), f32),
        ),
        in_specs=[vmem, vmem, vmem, anywhere, anywhere, vmem, vmem, vmem],
        out_specs=(vmem, anywhere, anywhere, anywhere, anywhere),
        scratch_shapes=[
            pltpu.VMEM((units, width), bf16),
            pltpu.VMEM(w_out.shape, bf16),
            pltpu.VMEM((blocks,) + packed, bf16),
            pltpu.VMEM((blocks,) + packed, bf16),
            pltpu.VMEM((blocks,) + packed, bf16),
            pltpu.VMEM((blocks, 8, 128), jnp.int32),
            pltpu.VMEM((blocks - 1,) + packed, bf16),
            pltpu.VMEM((blocks - 1,) + packed, bf16),
            pltpu.VMEM((blocks - 1,) + packed, bf16),
            pltpu.VMEM((blocks - 1,) + packed, bf16),
            pltpu.VMEM((group, width), f32),
            pltpu.VMEM((group, width), f32),
            pltpu.VMEM((group, width), bf16),
            pltpu.VMEM((group, width), bf16),
            pltpu.VMEM((group, width), bf16),
            pltpu.VMEM((group, units), bf16),
            pltpu.VMEM((group, units), bf16),
            pltpu.VMEM((group, units), f32),
            pltpu.VMEM((groups, group, width), bf16),
            pltpu.VMEM((units, groups * group), bf16),
            pltpu.VMEM((units, groups * group), f32),
            dma((3,)),
            dma((2,)),
            dma((6, blocks - 1)),
            dma((6, blocks - 1)),
            dma((2, chips - 1)),
            dma((2, chips - 1)),
            dma((2, chips)),
            dma((2, chips)),
            dma((2,)),
        ],
        compiler_params=pltpu.CompilerParams(
            collective_id=0, has_side_effects=True, vmem_limit_bytes=58 * 1024 * 1024
        ),
    )(
        hidden_in, gain_mlp, gain_final, w_in.T, w_out, image_embeds, pair_ids[None, :],
        jnp.swapaxes(teacher_logits, 1, 2),
    )
    grad_w_in, grad_w_out = weight_grads(
        all_x.reshape(groups * group, width), all_r.reshape(groups * group, width), act_all, steep_all, w_out
    )
    return grad_hidden, grad_w_in, grad_w_out


def choose(*args):
    rows, width = args[0].shape
    units = args[3].shape[1]
    groups, blocks = lax.axis_size("dp"), lax.axis_size("blk")
    gathered = groups * blocks * rows * width * 2 * 2
    summed = width * units * 2 * 4
    fits = groups % 2 == 0 and groups > 2 and blocks > 1 and rows % 16 == 8 and rows > 16 and width % 128 == 0
    if fits and gathered <= summed:
        return gathered_device(*args)
    return per_device(*args)


def solution(mesh):
    in_specs = (
        P(("dp", "blk"), None),
        P(),
        P(),
        P(None, "blk"),
        P("blk", None),
        P(("dp", "blk"), None),
        P(("dp", "blk")),
        P("dp", None, "blk"),
    )
    out_specs = (P(("dp", "blk"), None), P(None, "blk"), P("blk", None))
    return jax.shard_map(
        choose, mesh=mesh, in_specs=in_specs, out_specs=out_specs, check_vma=False
    )
```
